512 devices in a mesh: dp: 16 (over x, y), expert: 32 (over z, core).
Axes of the slice: x: 4, y: 4, z: 16, core: 2. Of those that a mesh axis runs over, the one named last changes fastest.
Arguments:
- cotangent: bfloat16 [65536, 5120], P(('dp', 'expert')), may hold values from -6 to 6
- route_weights: float32 [65536, 6], P(('dp', 'expert')), may hold values from 0.05 to 1
- token_experts: int32 [65536, 6], P(('dp', 'expert')), may hold values from 0 to 159, as said below
- saved_hidden: bfloat16 [16, 32, 32, 16, 1536], P('dp', 'expert'), may hold values from -6 to 6
- previous_right: bfloat16 [32, 1536, 128], P('expert', 'dp'), may hold values from -8 to 8
Outputs:
- left_factor: float32 [32, 5120, 128], P('expert', 'dp')
- right_factor: float32 [32, 1536, 128], P('expert', 'dp')
The draws below stay inside these ranges and needn't reach their ends.
Inputs may be any that keep to these rules, and one draw needn't show every extreme that they name: `token_experts`: each token names 6 different experts. On one device at most 16 tokens name any one of the experts 0 to 31, and in every draw one of these experts is named by exactly 16 tokens on every device.
All inputs are finite; a program needn't handle non-finite values.
Results may differ from the reference program's by a relative error of at most 0.0049.
Values may be sent and summed in bfloat16 or wider, within the bound.
A program may use at most 64 MiB of HBM per device.

```python
import math
import jax
import jax.numpy as jnp
from jax import lax

D = 5120
FF = 1536
EXPERTS = 160
TOP = 6
RANK = 128
MOST = 16
TOK_DEV = 128
EXPERT_SPAN = 32
TOKENS = 65536
N_DP = 16
N_EXPERT = 32


def draw_token_experts(key, part):
    key = jax.random.fold_in(key, 11)
    random_subkeys = jax.random.split(key, 4)
    blocks = TOKENS // TOK_DEV
    favoured = jax.random.randint(random_subkeys[0], (), 0, EXPERT_SPAN)
    extra_boost = jax.random.randint(random_subkeys[1], (EXPERT_SPAN,), 400, 1400)
    opening = jax.random.randint(random_subkeys[2], (blocks, 1, EXPERT_SPAN), 0, TOK_DEV)
    router_scores = jax.random.randint(random_subkeys[3], (blocks, TOK_DEV, EXPERTS), 0, 1000)
    position = jnp.arange(TOK_DEV, dtype=jnp.int32)[None, :, None]
    allowed = (position - opening) % TOK_DEV < MOST
    within_range = router_scores[:, :, :EXPERT_SPAN] + extra_boost[None, None, :]
    within_range = jnp.where(jnp.arange(EXPERT_SPAN, dtype=jnp.int32)[None, None, :] == favoured, 1000000, within_range)
    within_range = jnp.where(allowed, within_range, -1000000)
    router_scores = jnp.concatenate([within_range, router_scores[:, :, EXPERT_SPAN:]], axis=2)
    router_scores = router_scores * 256 + jnp.arange(EXPERTS, dtype=jnp.int32)[None, None, :]
    ranked, chosen = lax.top_k(router_scores, TOP)
    return chosen.reshape(TOKENS, TOP).astype(jnp.int32)


def draw_previous_right(key, part):
    key = jax.random.fold_in(key, 23)
    random_subkeys = jax.random.split(key, 3)
    shared = jax.random.normal(random_subkeys[1], (EXPERT_SPAN, FF, 1), jnp.float32)
    mixing = jax.random.uniform(random_subkeys[2], (EXPERT_SPAN, 1, RANK), jnp.float32, 0.3, 0.8)
    noise = jax.random.normal(random_subkeys[0], (EXPERT_SPAN, FF, RANK), jnp.float32)
    return jnp.clip(noise + shared * mixing, -8.0, 8.0).astype(jnp.bfloat16)


def levels(own_key, shape, shards, low, top_value):
    def one(dim, blocks):
        draws = jax.random.uniform(jax.random.fold_in(jax.random.fold_in(own_key, 6), dim), (blocks,), jnp.float32, low / len(shards), top_value / len(shards))
        return jnp.repeat(jnp.exp(draws), shape[dim] // blocks).reshape((-1,) + (1,) * (len(shape) - dim - 1))

    gain = one(*shards[0])
    for cut in shards[1:]:
        gain = gain * one(*cut)
    return gain


def normal_values(rng, extent, width, bound, cuts=(), kind=jnp.bfloat16):
    drawn = jax.random.normal(rng, extent, jnp.float32) * width
    if len(cuts) > 0:
        drawn = levels(rng, extent, cuts, -0.22, 0.18) * drawn
    return jnp.clip(drawn, min=-bound, max=bound).astype(kind)


def setup_inputs(seed: int = 0) -> dict:
    key_of = jax.random.split(jax.random.key(seed), 6)
    cotangent = normal_values(key_of[0], (TOKENS, D), 1.0, 6.0, ((0, 512),))
    route_weights = jnp.clip(jnp.exp(math.log(1.0) - 2.9957323 * jax.random.uniform(key_of[1], (TOKENS, TOP), jnp.float32) ** levels(key_of[1], (TOKENS, TOP), ((0, 512),), -0.2, 0.2)), 0.05, 1.0)
    token_experts = draw_token_experts(jax.random.fold_in(key_of[5], 71), 0)
    saved_hidden = normal_values(key_of[3], (N_DP, EXPERT_SPAN, EXPERT_SPAN, MOST, FF), 1.0, 6.0, ((0, 16), (1, 32)))
    previous_right = draw_previous_right(jax.random.fold_in(key_of[5], 71), 0)
    return {"cotangent": cotangent, "route_weights": route_weights, "token_experts": token_experts, "saved_hidden": saved_hidden, "previous_right": previous_right}


EPSILON = 1e-06

def reference(cotangent, route_weights, token_experts, saved_hidden, previous_right):
    devices = N_DP * N_EXPERT
    cotangent_blocks = cotangent.reshape(devices, TOK_DEV, D)
    expert_blocks = token_experts.reshape(devices, TOK_DEV, TOP)
    weight_blocks = route_weights.reshape(devices, TOK_DEV, TOP)
    slot_range = jnp.arange(MOST, dtype=jnp.int32)
    token_range = jnp.arange(TOK_DEV, dtype=jnp.int32)

    def one_expert(expert):
        matches = expert_blocks == expert
        routed = jnp.any(matches, axis=2).astype(jnp.int32)
        weight_sum = lax.optimization_barrier(jnp.sum(jnp.where(matches, weight_blocks, 0.0), axis=2))
        slots = jnp.cumsum(routed, axis=1) - routed
        chosen = (routed[:, :, None] == 1) & (slots[:, :, None] == slot_range[None, None, :])
        source_row = lax.optimization_barrier(jnp.sum(jnp.where(chosen, token_range[None, :, None], 0), axis=1)).astype(jnp.int32)
        slot_weight = lax.optimization_barrier(jnp.sum(jnp.where(chosen, weight_sum[:, :, None], 0.0), axis=1))
        picked = jnp.take_along_axis(cotangent_blocks, source_row[:, :, None], axis=1)
        scaled_rows = (picked * slot_weight[:, :, None]).astype(jnp.bfloat16).reshape(devices * MOST, D)
        hidden_rows = lax.dynamic_index_in_dim(saved_hidden, expert, 1, keepdims=False).reshape(devices * MOST, FF)
        right_prev = lax.dynamic_index_in_dim(previous_right, expert, 0, keepdims=False)
        projected = jnp.dot(hidden_rows.astype(jnp.float32), right_prev.astype(jnp.float32), preferred_element_type=jnp.float32).astype(jnp.bfloat16)
        left_sum = jnp.dot(scaled_rows.T.astype(jnp.float32), projected.astype(jnp.float32), preferred_element_type=jnp.float32)
        basis, triangle = jnp.linalg.qr(left_sum)
        signs = jnp.where(jnp.diagonal(triangle) < 0, -1.0, 1.0)
        basis = basis * signs[None, :]
        rotated_factor = jnp.dot(scaled_rows.astype(jnp.float32), basis.astype(jnp.bfloat16).astype(jnp.float32), preferred_element_type=jnp.float32).astype(jnp.bfloat16)
        right_sum = jnp.dot(hidden_rows.T.astype(jnp.float32), rotated_factor.astype(jnp.float32), preferred_element_type=jnp.float32)
        column_sums = lax.optimization_barrier(jnp.sum(right_sum * right_sum, axis=0))
        left_out = basis * math.sqrt(D)
        right_out = right_sum * (math.sqrt(FF) / jnp.sqrt(column_sums + EPSILON))
        return (left_out, right_out)
    left_factor, right_factor = lax.map(one_expert, jnp.arange(N_EXPERT, dtype=jnp.int32))
    return (left_factor, right_factor)
```

```python
import functools
import math

import jax
import jax.numpy as jnp
from jax import lax
from jax.experimental import pallas as pl
from jax.experimental.pallas import tpu as pltpu
from jax.sharding import PartitionSpec as P

EPSILON = 1e-06
MESH = pl.DeviceIdType.MESH
F32 = jnp.float32
BF16 = jnp.bfloat16
HIGHEST = lax.Precision.HIGHEST


class Sizes:
    def __init__(self, n_dp, n_expert, tokens, width, capacity, hidden, rank, chunks):
        self.n_dp, self.n_expert = n_dp, n_expert
        self.n_z = n_expert // 2
        assert self.n_z == n_dp
        self.ny = int(round(math.sqrt(n_dp)))
        self.tokens, self.width, self.capacity = tokens, width, capacity
        self.hidden, self.rank, self.chunks = hidden, rank, chunks
        self.rows = n_expert * capacity
        self.wide = width // chunks
        self.piece = self.wide // self.n_z
        self.pair = 2 * capacity
        self.own_left = width // n_dp
        self.own_right = hidden // n_dp
        self.half = self.n_z // 2


def inverse_factor(gram_ref, inverse_ref, size):
    lane = lax.broadcasted_iota(jnp.int32, (size, size), 1)
    sub = lax.broadcasted_iota(jnp.int32, (size, size), 0)
    inverse_ref[...] = jnp.where(lane == sub, 1.0, 0.0).astype(F32)

    def step(j, carry):
        row = gram_ref[pl.ds(j, 1), :]
        inv_row = inverse_ref[pl.ds(j, 1), :]
        first = lax.broadcasted_iota(jnp.int32, (1, size), 1)
        pivot = jnp.sum(jnp.where(first == j, row, 0.0), axis=1, keepdims=True)
        gram = gram_ref[...]
        column = jnp.sum(jnp.where(lane == j, gram, 0.0), axis=1, keepdims=True)
        factor = jnp.where(sub[:, :1] > j, column / pivot, 0.0)
        gram_ref[...] = gram - factor * row
        inverse_ref[...] = inverse_ref[...] - factor * inv_row
        return carry

    lax.fori_loop(0, size, step, 0)
    pivots = jnp.sum(jnp.where(lane == sub, gram_ref[...], 0.0), axis=1, keepdims=True)
    inverse_ref[...] = inverse_ref[...] * lax.rsqrt(pivots)


def kernel(
    m,
    cot, weights, experts, hidden, previous,
    left_out, right_out,
    key_s, wsum_s, pick_s, scale_s,
    out_s, arr_s, prev_s, proj_s, turn_s, projected_s,
    part_s, from_left, from_right, own_s, full_s,
    gram_s, inverse_s, acc_s, rot_s, back_s, left_s, terms_s, landed_s, square_s, squares_s,
    row_send, row_recv, prev_sem, turn_sem, proj_sem,
    sum_right, sum_left, gat_right, gat_left, back_sem, left_sem, terms_sem, square_sem,
):
    i = lax.axis_index("dp")
    e = lax.axis_index("expert")
    z = lax.div(e, 2)
    c = lax.rem(e, 2)
    me = i * 2 + c
    K = m.chunks
    diagonal = i == z
    right_e = lax.rem(z + 1, m.n_z) * 2 + c
    left_e = lax.rem(z + m.n_z - 1, m.n_z) * 2 + c

    def peer(j):
        j = lax.rem(j * 11, 2 * m.n_dp)
        x = lax.rem(lax.div(i, m.ny) + lax.div(j, 2 * m.ny), m.ny)
        y = lax.rem(lax.rem(i, m.ny) + lax.rem(lax.div(j, 2), m.ny), m.ny)
        core = lax.rem(c + lax.rem(j, 2), 2)
        return x * m.ny + y, core

    def remote(src, dst, send, recv, to):
        return pltpu.make_async_remote_copy(
            src_ref=src, dst_ref=dst, send_sem=send, recv_sem=recv, device_id=to, device_id_type=MESH
        )

    def wait_bytes(ref, sem):
        pltpu.make_async_copy(ref, ref, sem).wait()

    barrier = pltpu.get_barrier_semaphore()

    def greet(to):
        pl.semaphore_signal(barrier, inc=1, device_id=to, device_id_type=MESH)

    @pl.loop(1, 2 * m.n_dp)
    def _(j):
        a, core = peer(j)
        greet((a, z * 2 + core))

    @pl.loop(1, m.n_z)
    def _(j):
        greet((i, lax.rem(z + j, m.n_z) * 2 + c))

    @pl.loop(0, m.n_dp)
    def _(j):
        @pl.when(jnp.logical_not(jnp.logical_and(diagonal, j == i)))
        def _():
            greet((j, i * 2 + c))

        @pl.when(jnp.logical_not(jnp.logical_and(diagonal, j == z)))
        def _():
            greet((z, j * 2 + c))

    ids = experts[...]
    values = weights[...]
    square = (m.tokens, m.tokens)
    lane = lax.broadcasted_iota(jnp.int32, square, 1)
    sub = lax.broadcasted_iota(jnp.int32, square, 0)
    wsum = jnp.zeros(square, F32)
    routed = jnp.zeros(square, F32)
    for t in range(ids.shape[1]):
        hit = ids[:, t : t + 1] == lane
        wsum = wsum + jnp.where(hit, values[:, t : t + 1], 0.0)
        routed = jnp.where(hit, 1.0, routed)
    wsum_s[...] = wsum.T[: m.n_expert]
    routed_t = routed.T[: m.n_expert]
    before = jnp.where(sub < lane, 1.0, 0.0).astype(BF16)
    slots = jnp.dot(routed_t.astype(BF16), before, preferred_element_type=F32)
    key_s[...] = jnp.where(routed_t > 0.0, slots, -1.0)

    @pl.loop(0, m.n_expert)
    def _(x):
        slot = lax.broadcasted_iota(jnp.int32, (m.capacity, m.tokens), 0).astype(F32)
        hit = key_s[pl.ds(x, 1), :] == slot
        rows = pl.ds(pl.multiple_of(x * m.capacity, m.capacity), m.capacity)
        pick_s[rows, :] = jnp.where(hit, 1.0, 0.0).astype(BF16)
        weight = jnp.sum(jnp.where(hit, wsum_s[pl.ds(x, 1), :], 0.0), axis=1, keepdims=True)
        scale_s[rows, :] = jnp.broadcast_to(weight, (m.capacity, m.tokens))

    def scale_rows(k):
        @pl.loop(0, m.wide // 128)
        def _(n):
            inside = pl.ds(pl.multiple_of(n * 128, 128), 128)
            whole = pl.ds(pl.multiple_of(k * m.wide + n * 128, 128), 128)
            picked = jnp.dot(pick_s[...], cot[:, whole], preferred_element_type=F32)
            out_s[k, :, inside] = (picked * scale_s[...]).astype(BF16)

    def rows_of(index, count):
        return pl.ds(pl.multiple_of(index * count, count), count)

    mine = rows_of(me, m.capacity)

    def send_rows(k):
        @pl.loop(1, 2 * m.n_dp)
        def _(j):
            a, core = peer(j)
            remote(
                out_s.at[k, rows_of(a * 2 + core, m.capacity)], arr_s.at[k, mine],
                row_send.at[k], row_recv.at[k], (a, z * 2 + core),
            ).start()

        arr_s[k, mine, :] = out_s[k, mine, :]

    scale_rows(0)
    pl.semaphore_wait(
        barrier, 2 * m.n_dp - 1 + m.n_z - 1 + 2 * m.n_dp - 2 * diagonal.astype(jnp.int32)
    )

    @pl.loop(1, m.n_dp)
    def _(j):
        remote(
            previous, prev_s.at[rows_of(i, m.own_right)],
            prev_sem.at[0], prev_sem.at[1], (lax.rem(i + j, m.n_dp), e),
        ).start()

    prev_s[rows_of(i, m.own_right), :] = previous[...]
    send_rows(0)
    others = (m.n_dp - 1) * m.own_right
    wait_bytes(prev_s.at[pl.ds(0, others)], prev_sem.at[1])

    proj_s[...] = jnp.dot(hidden[...], prev_s[...], preferred_element_type=F32).astype(BF16)

    @pl.loop(1, m.n_z)
    def _(j):
        to = lax.rem(z + j, m.n_z)
        remote(
            proj_s.at[rows_of(to, m.pair)], turn_s.at[rows_of(z, m.pair)],
            turn_sem.at[0], turn_sem.at[1], (i, to * 2 + c),
        ).start()

    turn_s[rows_of(z, m.pair), :] = proj_s[rows_of(z, m.pair), :]
    scale_rows(1)
    send_rows(1)
    most = pl.ds(0, (m.n_z - 1) * m.pair)
    wait_bytes(turn_s.at[most], turn_sem.at[1])

    @pl.loop(1, m.n_dp)
    def _(j):
        to = lax.rem(i + j, m.n_dp)
        remote(
            turn_s.at[rows_of(to, m.pair)], projected_s.at[rows_of(i, m.pair)],
            proj_sem.at[0], proj_sem.at[1], (to, e),
        ).start()

    projected_s[rows_of(i, m.pair), :] = turn_s[rows_of(i, m.pair), :]
    for k in range(2, K):
        scale_rows(k)
        send_rows(k)
    wait_bytes(projected_s.at[most], proj_sem.at[1])

    def piece_of(index):
        return rows_of(index, m.piece)

    def shifted(shift):
        return lax.rem(z + shift + 2 * m.n_z, m.n_z)

    def left_terms(k):
        @pl.loop(0, m.wide // 128)
        def _(n):
            inside = pl.ds(pl.multiple_of(n * 128, 128), 128)
            turned = lax.dot_general(
                projected_s[...], arr_s[k, :, inside], (((0,), (0,)), ((), ())),
                preferred_element_type=F32,
            )
            part_s[k, inside, :] = turned.T

    half = m.half

    def sum_copy(k, s, rightward, src):
        if rightward:
            return remote(src, from_left.at[k, s], sum_right.at[0, k, s], sum_right.at[1, k, s], (i, right_e))
        return remote(src, from_right.at[k, s], sum_left.at[0, k, s], sum_left.at[1, k, s], (i, left_e))

    def sum_first(k):
        sum_copy(k, 0, True, part_s.at[k, piece_of(shifted(half))]).start()
        sum_copy(k, 0, False, part_s.at[k, piece_of(shifted(1 - half))]).start()

    def sum_step(k, s):
        wait_bytes(from_left.at[k, s - 1], sum_right.at[1, k, s - 1])
        from_left[k, s - 1] = from_left[k, s - 1] + part_s[k, piece_of(shifted(half - s)), :]
        sum_copy(k, s, True, from_left.at[k, s - 1]).start()

        @pl.when(s < half - 1)
        def _():
            wait_bytes(from_right.at[k, s - 1], sum_left.at[1, k, s - 1])
            from_right[k, s - 1] = from_right[k, s - 1] + part_s[k, piece_of(shifted(1 - half + s)), :]
            sum_copy(k, s, False, from_right.at[k, s - 1]).start()

    def sum_last(k):
        wait_bytes(from_left.at[k, half - 1], sum_right.at[1, k, half - 1])
        wait_bytes(from_right.at[k, half - 2], sum_left.at[1, k, half - 2])
        total = part_s[k, piece_of(z), :] + from_left[k, half - 1] + from_right[k, half - 2]
        own_s[k] = total
        full_s[k, piece_of(z), :] = total.astype(BF16)

    def gather_copy(k, s, rightward):
        if rightward:
            block = full_s.at[k, piece_of(shifted(-s))]
            return remote(block, block, gat_right.at[0, k, s], gat_right.at[1, k, s], (i, right_e))
        block = full_s.at[k, piece_of(shifted(s))]
        return remote(block, block, gat_left.at[0, k, s], gat_left.at[1, k, s], (i, left_e))

    def gather_first(k):
        gather_copy(k, 0, True).start()
        gather_copy(k, 0, False).start()

    def gather_step(k, s):
        wait_bytes(full_s.at[k, piece_of(shifted(-s))], gat_right.at[1, k, s - 1])
        gather_copy(k, s, True).start()

        @pl.when(s < half - 1)
        def _():
            wait_bytes(full_s.at[k, piece_of(shifted(s))], gat_left.at[1, k, s - 1])
            gather_copy(k, s, False).start()

    def gather_last(k):
        wait_bytes(full_s.at[k, piece_of(shifted(-half))], gat_right.at[1, k, half - 1])
        wait_bytes(full_s.at[k, piece_of(shifted(half - 1))], gat_left.at[1, k, half - 2])

    gram_s[...] = jnp.zeros_like(gram_s)
    acc_s[...] = jnp.zeros_like(acc_s)

    def use_chunk(k):
        whole = full_s[k]
        gram_s[...] += lax.dot_general(
            whole, whole, (((0,), (0,)), ((), ())), preferred_element_type=F32
        )
        acc_s[...] += jnp.dot(arr_s[k], whole, preferred_element_type=F32)

    all_rows = pl.ds(0, (2 * m.n_dp - 1) * m.capacity)
    for k in range(K):
        wait_bytes(arr_s.at[k, all_rows], row_recv.at[k])
        left_terms(k)
        sum_first(k)
        if k > 0:
            gather_first(k - 1)

        @pl.loop(1, half)
        def _(s):
            sum_step(k, s)
            if k > 0:
                gather_step(k - 1, s)

        sum_last(k)
        if k > 0:
            gather_last(k - 1)
            use_chunk(k - 1)
    gather_first(K - 1)

    @pl.loop(1, half)
    def _(s):
        gather_step(K - 1, s)

    gather_last(K - 1)
    use_chunk(K - 1)

    inverse_factor(gram_s, inverse_s, m.rank)
    upper_inverse = inverse_s[...].T

    rot_s[...] = jnp.dot(
        acc_s[...], upper_inverse, precision=HIGHEST, preferred_element_type=F32
    ).astype(BF16)

    @pl.loop(0, m.n_dp)
    def _(j):
        to = lax.rem(i + j, m.n_dp)

        @pl.when(jnp.logical_not(jnp.logical_and(diagonal, to == i)))
        def _():
            remote(
                rot_s.at[rows_of(to, m.pair)], back_s.at[rows_of(z, m.pair)],
                back_sem.at[0], back_sem.at[1], (to, i * 2 + c),
            ).start()

    for k in range(K):
        left_s[k] = math.sqrt(m.width) * jnp.dot(
            own_s[k], upper_inverse, precision=HIGHEST, preferred_element_type=F32
        )

    def left_place(k):
        index = k * m.n_z + z
        return lax.div(index, K), rows_of(lax.rem(index, K), m.piece)

    def left_here(k):
        return jnp.logical_and(diagonal, left_place(k)[0] == i)

    for k in range(K):
        to, place = left_place(k)

        @pl.when(left_here(k))
        def _():
            left_out[place, :] = left_s[k]

        @pl.when(jnp.logical_not(left_here(k)))
        def _():
            remote(
                left_s.at[k], left_out.at[place], left_sem.at[0, k], left_sem.at[1, lax.rem(k * m.n_z + z, K)],
                (to, i * 2 + c),
            ).start()

    @pl.when(diagonal)
    def _():
        back_s[rows_of(z, m.pair), :] = rot_s[rows_of(i, m.pair), :]
        wait_bytes(back_s.at[most], back_sem.at[1])
        wait_bytes(rot_s.at[most], back_sem.at[0])

    @pl.when(jnp.logical_not(diagonal))
    def _():
        wait_bytes(back_s, back_sem.at[1])
        wait_bytes(rot_s, back_sem.at[0])

    @pl.loop(0, m.hidden // 128)
    def _(n):
        inside = pl.ds(pl.multiple_of(n * 128, 128), 128)
        turned = lax.dot_general(
            back_s[...], hidden[:, inside], (((0,), (0,)), ((), ())), preferred_element_type=F32
        )
        terms_s[inside, :] = turned.T

    @pl.loop(1, m.n_dp)
    def _(j):
        to = lax.rem(i + j, m.n_dp)
        remote(
            terms_s.at[rows_of(to, m.own_right)], landed_s.at[rows_of(i, m.own_right)],
            terms_sem.at[0], terms_sem.at[1], (to, e),
        ).start()

    landed_s[rows_of(i, m.own_right), :] = terms_s[rows_of(i, m.own_right), :]
    wait_bytes(landed_s.at[pl.ds(0, others)], terms_sem.at[1])
    right = landed_s[0 : m.own_right, :]
    for n in range(1, m.n_dp):
        right = right + landed_s[n * m.own_right : (n + 1) * m.own_right, :]
    square_s[...] = jnp.broadcast_to(jnp.sum(right * right, axis=0, keepdims=True), square_s.shape)

    @pl.loop(1, m.n_dp)
    def _(j):
        to = lax.rem(i + j, m.n_dp)
        remote(
            square_s, squares_s.at[rows_of(i, 8)], square_sem.at[0], square_sem.at[1], (to, e)
        ).start()

    squares_s[rows_of(i, 8), :] = square_s[...]
    wait_bytes(squares_s.at[pl.ds(0, (m.n_dp - 1) * 8)], square_sem.at[1])
    total = squares_s[0:1, :]
    for n in range(1, m.n_dp):
        total = total + squares_s[n * 8 : n * 8 + 1, :]
    right_out[...] = right * (math.sqrt(m.hidden) / jnp.sqrt(total + EPSILON))

    for k in range(K):
        wait_bytes(out_s.at[k, all_rows], row_send.at[k])

        @pl.loop(0, half)
        def _(s):
            wait_bytes(from_left.at[k, s], sum_right.at[0, k, s])
            wait_bytes(full_s.at[k, piece_of(0)], gat_right.at[0, k, s])

            @pl.when(s < half - 1)
            def _():
                wait_bytes(from_right.at[k, s], sum_left.at[0, k, s])
                wait_bytes(full_s.at[k, piece_of(0)], gat_left.at[0, k, s])

        @pl.when(jnp.logical_not(left_here(k)))
        def _():
            wait_bytes(left_s.at[k], left_sem.at[0, k])

        index = i * K + k
        source = lax.rem(index, m.n_z)

        @pl.when(jnp.logical_not(jnp.logical_and(diagonal, source == z)))
        def _():
            wait_bytes(left_s.at[k], left_sem.at[1, k])

    wait_bytes(prev_s.at[pl.ds(0, others)], prev_sem.at[0])
    wait_bytes(turn_s.at[most], turn_sem.at[0])
    wait_bytes(projected_s.at[most], proj_sem.at[0])
    wait_bytes(landed_s.at[pl.ds(0, others)], terms_sem.at[0])
    wait_bytes(squares_s.at[pl.ds(0, (m.n_dp - 1) * 8)], square_sem.at[0])


def local(chunks, cotangent, route_weights, token_experts, saved_hidden, previous_right):
    n_dp, n_expert = lax.axis_size("dp"), lax.axis_size("expert")
    tokens, width = cotangent.shape
    capacity, hidden = saved_hidden.shape[3:]
    rank = previous_right.shape[2]
    m = Sizes(n_dp, n_expert, tokens, width, capacity, hidden, rank, chunks)
    K, half = m.chunks, m.half
    vmem = pl.BlockSpec(memory_space=pltpu.VMEM)
    dma = pltpu.SemaphoreType.DMA
    left, right = pl.pallas_call(
        functools.partial(kernel, m),
        out_shape=(
            jax.ShapeDtypeStruct((m.own_left, rank), F32),
            jax.ShapeDtypeStruct((m.own_right, rank), F32),
        ),
        in_specs=[vmem] * 5,
        out_specs=(vmem, vmem),
        scratch_shapes=[
            pltpu.VMEM((n_expert, tokens), F32),
            pltpu.VMEM((n_expert, tokens), F32),
            pltpu.VMEM((m.rows, tokens), BF16),
            pltpu.VMEM((m.rows, tokens), F32),
            pltpu.VMEM((K, m.rows, m.wide), BF16),
            pltpu.VMEM((K, m.rows, m.wide), BF16),
            pltpu.VMEM((hidden, rank), BF16),
            pltpu.VMEM((m.rows, rank), BF16),
            pltpu.VMEM((m.rows, rank), BF16),
            pltpu.VMEM((m.rows, rank), BF16),
            pltpu.VMEM((K, m.wide, rank), F32),
            pltpu.VMEM((K, half, m.piece, rank), F32),
            pltpu.VMEM((K, half, m.piece, rank), F32),
            pltpu.VMEM((K, m.piece, rank), F32),
            pltpu.VMEM((K, m.wide, rank), BF16),
            pltpu.VMEM((rank, rank), F32),
            pltpu.VMEM((rank, rank), F32),
            pltpu.VMEM((m.rows, rank), F32),
            pltpu.VMEM((m.rows, rank), BF16),
            pltpu.VMEM((m.rows, rank), BF16),
            pltpu.VMEM((K, m.piece, rank), F32),
            pltpu.VMEM((hidden, rank), F32),
            pltpu.VMEM((hidden, rank), F32),
            pltpu.VMEM((8, rank), F32),
            pltpu.VMEM((8 * n_dp, rank), F32),
            dma((K,)),
            dma((K,)),
            dma((2,)),
            dma((2,)),
            dma((2,)),
            dma((2, K, half)),
            dma((2, K, half)),
            dma((2, K, half)),
            dma((2, K, half)),
            dma((2,)),
            dma((2, K)),
            dma((2,)),
            dma((2,)),
        ],
        compiler_params=pltpu.CompilerParams(
            collective_id=1, has_side_effects=True, vmem_limit_bytes=48 * 2**20
        ),
    )(
        cotangent, route_weights, token_experts,
        saved_hidden.reshape(m.rows, hidden), previous_right[0],
    )
    return (left[None], right[None])


def solution(mesh, chunks=5):
    in_specs = (
        P(("dp", "expert"), None),
        P(("dp", "expert"), None),
        P(("dp", "expert"), None),
        P("dp", "expert", None, None, None),
        P("expert", "dp", None),
    )
    out_specs = (P("expert", "dp", None), P("expert", "dp", None))
    return jax.shard_map(
        functools.partial(local, chunks), mesh=mesh, in_specs=in_specs, out_specs=out_specs, check_vma=False
    )
```
